32 devices in a mesh: groups: 2 (over x), seq: 16 (over z, y, core).
Axes of the slice: x: 2, y: 2, z: 4, core: 2. Of those that a mesh axis runs over, the one named last changes fastest.
Arguments:
- activations: bfloat16 [4096, 8192], P(('groups', 'seq')), parts along dimension 0, may hold values from -6 to 6
- out_grads: bfloat16 [4096, 14336], P(('groups', 'seq')), parts along dimension 0, may hold values from -6 to 6
- query_grad: bfloat16 [2, 16384, 14336], P(None, ('groups', 'seq')), parts along dimension 1, may hold values from -0.00015258789 to 0.00015258789
- segment_ids: int32 [32, 128], P(('groups', 'seq')), parts along dimension 0, may hold values from 0 to 3, never falling along the last dimension, each value on 1 to 64 neighbouring positions
- sequence_ids: int32 [32, 4], P(('groups', 'seq')), parts along dimension 0, may hold values from 0 to 31
Outputs:
- scores: float32 [2, 64], P(None, ('groups', 'seq')), parts along dimension 1
The draws below stay inside these ranges and needn't reach their ends.
There are 2 independent parts, one for each index of `groups`. The reference program is written for one: setup_inputs(seed, part) draws one part's arguments, and reference() takes and returns one part's arrays. A program takes and returns all parts, laid end to end along the dimension named above; each array names one. Nothing has to cross between parts.
All inputs are finite; a program needn't handle non-finite values.
Results may differ from the reference program's by a relative error of at most 0.0003.
Values may be sent and summed in bfloat16 or wider, within the bound.
A program may use at most 192 MiB of HBM per device.

```python
import math
import jax
import jax.numpy as jnp
import numpy as np
from jax import lax

D = 8192
FF = 14336
NQ = 2
TOK_DEV = 128
SEGS = 4
SEQS_DEV = 2
TOKENS = 2048
NSEQ_TR = 32
N_SEQ = 16


def plant(array, key, low, high):
    place = [jax.random.randint(jax.random.fold_in(key, axis), (), 0, length) for axis, length in enumerate(array.shape)]
    longest = array.shape.index(max(array.shape))
    neighbour = place[:longest] + [(place[longest] + 1) % array.shape[longest]] + place[longest + 1:]
    return array.at[tuple(place)].set(low).at[tuple(neighbour)].set(high)


def levels(key, extent, shards, low, largest):
    level, own = 1.0, jax.random.fold_in(key, 6)
    for dim, shards_of in shards:
        steps = jnp.exp(jax.random.uniform(jax.random.fold_in(own, dim), (shards_of,), jnp.float32, low / len(shards), largest / len(shards)))
        level = level * jnp.repeat(steps, extent[dim] // shards_of).reshape([-1 if axis == dim else 1 for axis in range(len(extent))])
    return level


def length_profile(amount, total, limit, slope):
    weights = [(1 << 20) // math.isqrt(grade ** slope) + 1 for grade in range(2, amount + 1)]
    rest, counts = total - limit - (amount - 1), [1] * (amount - 1)
    while rest > 0:
        candidates = [i for i in range(amount - 1) if counts[i] < limit]
        whole, remaining = sum([weights[i] for i in candidates]), rest
        for i in candidates:
            extra = min(limit - counts[i], max(1, remaining * weights[i] // whole), rest)
            counts[i] = counts[i] + extra
            rest = rest - extra
    return np.array([limit] + counts)


def ragged(key, amount, total, reach, slope):
    if amount == 2:
        one = jax.random.randint(key, (), max(1, total - reach), min(reach, total - 1) + 1)
        return jnp.stack([one, total - one])
    lengths = jnp.asarray(length_profile(amount, total, reach, slope), jnp.int32)
    couples = (amount - 1) // 2
    giver, sink = lengths[1:1 + 2 * couples:2], lengths[2:2 + 2 * couples:2]
    room = jnp.minimum(giver - 1, reach - sink)
    moved = jax.random.randint(jax.random.fold_in(key, 1), (couples,), 0, 1 << 20) % (room + 1)
    lengths = lengths.at[1:1 + 2 * couples:2].set(giver - moved).at[2:2 + 2 * couples:2].set(sink + moved)
    return lengths[jax.random.permutation(jax.random.fold_in(key, 2), amount)]


def gaussian(key, shape, scale, limit, pieces=(), held_as=jnp.bfloat16):
    loudness = levels(key, shape, pieces, -0.22, 0.18) if pieces else 1.0
    result = jax.random.normal(key, shape, jnp.float32) * scale * loudness
    return jnp.minimum(jnp.maximum(result, -limit), limit).astype(held_as)


def setup_inputs(seed: int = 0, part: int = 0) -> dict:
    splits = jax.random.split(jax.random.key(seed), 6)
    part_splits = jax.random.split(jax.random.fold_in(splits[5], part), 6)
    return {
        "activations": gaussian(part_splits[0], (TOKENS, D), 1.0, 6.0, ((0, 16),)),
        "out_grads": gaussian(part_splits[1], (TOKENS, FF), 1.0, 6.0, ((0, 16),)),
        "query_grad": gaussian(part_splits[2], (NQ, D, FF), (FF * 3 * (D // N_SEQ) * 2 * (TOK_DEV // SEGS)) ** -0.5, 0.00015258789, ((1, 16),)),
        "segment_ids": jax.vmap(lambda own: jnp.searchsorted(jnp.cumsum(ragged(own, SEGS, TOK_DEV, TOK_DEV // 2, 1)), jnp.arange(TOK_DEV), side="right"))(jax.random.split(part_splits[3], N_SEQ)).reshape((N_SEQ, TOK_DEV)).astype(jnp.int32),
        "sequence_ids": plant(jax.random.randint(part_splits[4], (N_SEQ, SEGS), 0, NSEQ_TR), jax.random.fold_in(part_splits[4], 1), 0, NSEQ_TR - 1).astype(jnp.int32),
    }


def reference(activations, out_grads, query_grad, segment_ids, sequence_ids):
    band_rows = D // N_SEQ
    total = SEQS_DEV * N_SEQ
    acts_blocks = activations.reshape(N_SEQ, TOK_DEV, D)
    grad_blocks = out_grads.reshape(N_SEQ, TOK_DEV, FF)

    def one_block(inputs):
        block, acts, grads, segs, seqids = inputs
        grads32 = grads.astype(jnp.float32)
        partial_value = jnp.zeros((NQ, TOK_DEV), jnp.float32)
        for step in range(3):
            band = (block - step) % N_SEQ
            start = (band * band_rows).astype(jnp.int32)
            cols = lax.dynamic_slice_in_dim(acts, start, band_rows, 1)
            rows_list = []
            for query in range(NQ):
                rows = lax.dynamic_slice_in_dim(query_grad[query], start, band_rows, 0)
                h = jnp.dot(cols, rows, preferred_element_type=jnp.float32)
                rows_list.append(jnp.sum(h * grads32, axis=1))
            partial_value = partial_value + jnp.stack(rows_list)
        seg_hot = (segs[:, None] == jnp.arange(SEGS, dtype=jnp.int32)[None, :]).astype(jnp.float32)
        seq_hot = (seqids[:, None] == jnp.arange(total, dtype=jnp.int32)[None, :]).astype(jnp.float32)
        member = jnp.dot(seg_hot, seq_hot, precision=lax.Precision.HIGHEST)
        return jnp.dot(partial_value, member, precision=lax.Precision.HIGHEST)

    blocks = jnp.arange(N_SEQ, dtype=jnp.int32)
    terms = lax.map(one_block, (blocks, acts_blocks, grad_blocks, segment_ids, sequence_ids))
    return jnp.sum(terms, axis=0)
```

```python
import functools
import math

import jax
import jax.numpy as jnp
from jax import lax
from jax.experimental import pallas as pl
from jax.experimental.pallas import tpu as pltpu
from jax.sharding import PartitionSpec as P

SEGS = 4
SEQS_DEV = 2
MESH = pl.DeviceIdType.MESH


def kernel(
    count,
    chunk,
    act_ref,
    grad_ref,
    query_ref,
    seg_ref,
    seq_ref,
    out_ref,
    held_query,
    held_grad,
    held_act,
    held_sid,
    acc,
    term_mine,
    term_got,
    query_sem,
    own_sem,
    act_sem,
    far_send,
    far_recv,
    near_send,
    near_recv,
    side_send,
    side_recv,
    term_send,
    term_recv,
):
    group = lax.axis_index("groups")
    me = lax.axis_index("seq")
    queries, band, width = query_ref.shape
    tokens = grad_ref.shape[0]
    chunks = width // chunk
    pad = term_mine.shape[1]
    even = lax.rem(me, 2) == 0
    back1 = lax.rem(me + count - 1, count)
    back2 = lax.rem(me + count - 2, count)
    ahead1 = lax.rem(me + 1, count)

    def columns(owner):
        return act_ref.at[:, pl.ds(pl.multiple_of(owner * band, band), band)]

    def span(k):
        return pl.ds(pl.multiple_of(k * chunk, chunk), chunk)

    def query_copy(k):
        return pltpu.make_async_copy(
            query_ref.at[:, :, span(k)], held_query.at[k], query_sem.at[k]
        )

    def own_copy(k):
        return pltpu.make_async_copy(grad_ref.at[:, span(k)], held_grad.at[0, k], own_sem.at[k])

    def far_copy(k):
        return pltpu.make_async_remote_copy(
            src_ref=grad_ref.at[:, span(k)],
            dst_ref=held_grad.at[2, k],
            send_sem=far_send.at[k],
            recv_sem=far_recv.at[k],
            device_id=(group, back2),
            device_id_type=MESH,
        )

    def near_copy(k):
        return pltpu.make_async_remote_copy(
            src_ref=grad_ref.at[:, span(k)],
            dst_ref=held_grad.at[1, k],
            send_sem=near_send.at[k],
            recv_sem=near_recv.at[k],
            device_id=(group, back1),
            device_id_type=MESH,
        )

    def relay_copy(k):
        return pltpu.make_async_remote_copy(
            src_ref=held_grad.at[2, k],
            dst_ref=held_grad.at[1, k],
            send_sem=near_send.at[k],
            recv_sem=near_recv.at[k],
            device_id=(group, ahead1),
            device_id_type=MESH,
        )

    def side_copies():
        made = []
        for slot, target in ((1, back1), (2, back2)):
            for kind, source, place in (
                (0, columns(target), held_act.at[slot]),
                (1, held_sid.at[0], held_sid.at[slot]),
            ):
                index = 2 * (slot - 1) + kind
                made.append(
                    pltpu.make_async_remote_copy(
                        src_ref=source,
                        dst_ref=place,
                        send_sem=side_send.at[index],
                        recv_sem=side_recv.at[index],
                        device_id=(group, target),
                        device_id_type=MESH,
                    )
                )
        return made

    def term_copy(d):
        return pltpu.make_async_remote_copy(
            src_ref=term_mine,
            dst_ref=term_got.at[d],
            send_sem=term_send.at[d],
            recv_sem=term_recv.at[d],
            device_id=(group, lax.rem(me + d, count)),
            device_id_type=MESH,
        )

    barrier = pltpu.get_barrier_semaphore()

    @pl.loop(1, count)
    def _(d):
        pl.semaphore_signal(
            barrier,
            inc=1,
            device_id=(group, lax.rem(me + d, count)),
            device_id_type=MESH,
        )

    sid = jnp.zeros((1, tokens), jnp.int32)
    for s in range(SEGS):
        sid = sid + jnp.where(seg_ref[...] == s, seq_ref[0, s], 0)
    held_sid[0] = jnp.broadcast_to(sid.astype(jnp.float32), held_sid.shape[1:])
    acc[...] = jnp.zeros_like(acc)
    pl.semaphore_wait(barrier, count - 1)

    @pl.loop(0, chunks)
    def _(k):
        far_copy(k).start()

    @pl.when(lax.rem(me, 2) == 1)
    def _():
        @pl.loop(0, chunks)
        def _(k):
            near_copy(k).start()

    for copy in side_copies():
        copy.start()
    own_act = pltpu.make_async_copy(columns(me), held_act.at[0], act_sem)
    own_act.start()

    @pl.loop(0, chunks)
    def _(k):
        query_copy(k).start()
        own_copy(k).start()

    def add(k, slot):
        for q in range(queries):
            acc[slot, q] += lax.dot_general(
                held_grad[slot, k],
                held_query[k, q],
                (((1,), (1,)), ((), ())),
                preferred_element_type=jnp.float32,
            )

    @pl.loop(0, chunks)
    def _(k):
        query_copy(k).wait()
        own_copy(k).wait()
        add(k, 0)
        far_copy(k).wait_recv()

        @pl.when(even)
        def _():
            relay_copy(k).start()

        add(k, 2)
        near_copy(k).wait_recv()
        add(k, 1)

    own_act.wait()
    for copy in side_copies():
        copy.wait_recv()
    lanes = lax.broadcasted_iota(jnp.int32, (tokens, pad), 1).astype(jnp.float32)
    rows = [jnp.zeros((1, pad), jnp.float32) for _ in range(queries)]
    for slot in range(3):
        ids = jnp.broadcast_to(held_sid[slot][0:1, :], (tokens, tokens)).T
        member = (lanes == ids[:, 0:1]).astype(jnp.float32)
        act = held_act[slot].astype(jnp.float32)
        for q in range(queries):
            value = jnp.sum(acc[slot, q] * act, axis=1, keepdims=True)
            rows[q] = rows[q] + jnp.sum(value * member, axis=0, keepdims=True)
    sub = lax.broadcasted_iota(jnp.int32, term_mine.shape, 0)
    mine = jnp.zeros(term_mine.shape, jnp.float32)
    for q in range(queries):
        mine = jnp.where(sub == q, jnp.broadcast_to(rows[q], term_mine.shape), mine)
    term_mine[...] = mine

    @pl.loop(1, count)
    def _(d):
        term_copy(d).start()

    @pl.loop(0, chunks)
    def _(k):
        far_copy(k).wait_send()
        near_copy(k).wait_send()

    for copy in side_copies():
        copy.wait_send()

    def gather(d, total):
        term_copy(d).wait_recv()
        return total + term_got[d]

    total = lax.fori_loop(1, count, gather, term_mine[...])
    lane = lax.broadcasted_iota(jnp.int32, total.shape, 1)
    spot = lax.broadcasted_iota(jnp.int32, out_ref.shape, 1)
    result = jnp.zeros(out_ref.shape, jnp.float32)
    for s in range(SEQS_DEV):
        picked = jnp.sum(
            jnp.where(lane == me * SEQS_DEV + s, total, 0.0), axis=1, keepdims=True
        )
        result = jnp.where(
            spot == s, jnp.broadcast_to(picked[:queries], out_ref.shape), result
        )
    out_ref[...] = result

    @pl.loop(1, count)
    def _(d):
        term_copy(d).wait_send()


def local(activations, out_grads, query_grad, segment_ids, sequence_ids):
    count = lax.axis_size("seq")
    queries, band, width = query_grad.shape
    tokens = out_grads.shape[0]
    chunk = math.gcd(width, 1024)
    chunks = width // chunk
    pad = -(-SEQS_DEV * count // 128) * 128
    sub = -(-queries // 8) * 8
    dma = pltpu.SemaphoreType.DMA
    whole = pl.BlockSpec(memory_space=pl.ANY)
    return pl.pallas_call(
        functools.partial(kernel, count, chunk),
        out_shape=jax.ShapeDtypeStruct((queries, SEQS_DEV), jnp.float32),
        in_specs=[
            whole,
            whole,
            whole,
            pl.BlockSpec(memory_space=pltpu.VMEM),
            pl.BlockSpec(memory_space=pltpu.SMEM),
        ],
        out_specs=pl.BlockSpec(memory_space=pltpu.VMEM),
        scratch_shapes=[
            pltpu.VMEM((chunks, queries, band, chunk), jnp.bfloat16),
            pltpu.VMEM((3, chunks, tokens, chunk), jnp.bfloat16),
            pltpu.VMEM((3, tokens, band), jnp.bfloat16),
            pltpu.VMEM((3, 8, tokens), jnp.float32),
            pltpu.VMEM((3, queries, tokens, band), jnp.float32),
            pltpu.VMEM((sub, pad), jnp.float32),
            pltpu.VMEM((count, sub, pad), jnp.float32),
            dma((chunks,)),
            dma((chunks,)),
            dma,
            dma((chunks,)),
            dma((chunks,)),
            dma((chunks,)),
            dma((chunks,)),
            dma((4,)),
            dma((4,)),
            dma((count,)),
            dma((count,)),
        ],
        compiler_params=pltpu.CompilerParams(
            collective_id=0, has_side_effects=True, vmem_limit_bytes=56 * 1024 * 1024
        ),
        cost_estimate=pl.CostEstimate(
            flops=6 * queries * tokens * band * width,
            bytes_accessed=2 * queries * band * width,
            transcendentals=0,
        ),
    )(activations, out_grads, query_grad, segment_ids, sequence_ids)


def solution(mesh):
    placed = (
        P(("groups", "seq"), None),
        P(("groups", "seq"), None),
        P(None, ("groups", "seq"), None),
        P(("groups", "seq"), None),
        P(("groups", "seq"), None),
    )
    return jax.shard_map(
        local, mesh=mesh, in_specs=placed, out_specs=P(None, ("groups", "seq")), check_vma=False
    )
```

```python
import functools
import math

import jax
import jax.numpy as jnp
from jax import lax
from jax.experimental import pallas as pl
from jax.experimental.pallas import tpu as pltpu
from jax.sharding import PartitionSpec as P

SEGS = 4
SEQS_DEV = 2
MESH = pl.DeviceIdType.MESH


def kernel(
    count,
    chunk,
    act_ref,
    grad_ref,
    query_ref,
    seg_ref,
    seq_ref,
    out_ref,
    held_query,
    held_grad,
    held_act,
    held_sid,
    held_seg,
    held_seq,
    acc,
    term_mine,
    term_got,
    query_sem,
    own_sem,
    act_sem,
    id_sem,
    far_send,
    far_recv,
    near_send,
    near_recv,
    side_send,
    side_recv,
    term_send,
    term_recv,
):
    group = lax.axis_index("groups")
    me = lax.axis_index("seq")
    queries, band, width = query_ref.shape
    tokens = grad_ref.shape[0]
    chunks = width // chunk
    pad = term_mine.shape[1]
    even = lax.rem(me, 2) == 0
    back1 = lax.rem(me + count - 1, count)
    back2 = lax.rem(me + count - 2, count)
    ahead1 = lax.rem(me + 1, count)

    def columns(owner):
        return act_ref.at[:, pl.ds(pl.multiple_of(owner * band, band), band)]

    def span(k):
        return pl.ds(pl.multiple_of(k * chunk, chunk), chunk)

    def query_copy(k):
        return pltpu.make_async_copy(
            query_ref.at[:, :, span(k)], held_query.at[k], query_sem.at[k]
        )

    def own_copy(k):
        return pltpu.make_async_copy(grad_ref.at[:, span(k)], held_grad.at[0, k], own_sem.at[k])

    def far_copy(k):
        return pltpu.make_async_remote_copy(
            src_ref=grad_ref.at[:, span(k)],
            dst_ref=held_grad.at[2, k],
            send_sem=far_send.at[k],
            recv_sem=far_recv.at[k],
            device_id=(group, back2),
            device_id_type=MESH,
        )

    def near_copy(k):
        return pltpu.make_async_remote_copy(
            src_ref=grad_ref.at[:, span(k)],
            dst_ref=held_grad.at[1, k],
            send_sem=near_send.at[k],
            recv_sem=near_recv.at[k],
            device_id=(group, back1),
            device_id_type=MESH,
        )

    def relay_copy(k):
        return pltpu.make_async_remote_copy(
            src_ref=held_grad.at[2, k],
            dst_ref=held_grad.at[1, k],
            send_sem=near_send.at[k],
            recv_sem=near_recv.at[k],
            device_id=(group, ahead1),
            device_id_type=MESH,
        )

    def side_copies():
        made = []
        for slot, target in ((1, back1), (2, back2)):
            for kind, source, place in (
                (0, columns(target), held_act.at[slot]),
                (1, held_sid.at[0], held_sid.at[slot]),
            ):
                index = 2 * (slot - 1) + kind
                made.append(
                    pltpu.make_async_remote_copy(
                        src_ref=source,
                        dst_ref=place,
                        send_sem=side_send.at[index],
                        recv_sem=side_recv.at[index],
                        device_id=(group, target),
                        device_id_type=MESH,
                    )
                )
        return made

    def term_copy(d):
        return pltpu.make_async_remote_copy(
            src_ref=term_mine,
            dst_ref=term_got.at[d],
            send_sem=term_send.at[d],
            recv_sem=term_recv.at[d],
            device_id=(group, lax.rem(me + d, count)),
            device_id_type=MESH,
        )

    barrier = pltpu.get_barrier_semaphore()
    for d in range(1, count):
        pl.semaphore_signal(
            barrier,
            inc=1,
            device_id=(group, lax.rem(me + d, count)),
            device_id_type=MESH,
        )
    seg_copy = pltpu.make_async_copy(seg_ref, held_seg, id_sem.at[0])
    seq_copy = pltpu.make_async_copy(seq_ref, held_seq, id_sem.at[1])
    seg_copy.start()
    seq_copy.start()
    pl.semaphore_wait(barrier, count - 1)

    @pl.loop(0, chunks)
    def _(k):
        far_copy(k).start()

    @pl.when(lax.rem(me, 2) == 1)
    def _():
        @pl.loop(0, chunks)
        def _(k):
            near_copy(k).start()

    @pl.loop(0, chunks)
    def _(k):
        query_copy(k).start()
        own_copy(k).start()

    own_act = pltpu.make_async_copy(columns(me), held_act.at[0], act_sem)
    own_act.start()
    seg_copy.wait()
    seq_copy.wait()
    sid = jnp.zeros((1, tokens), jnp.int32)
    for s in range(SEGS):
        sid = sid + jnp.where(held_seg[...] == s, held_seq[0, s], 0)
    held_sid[0] = jnp.broadcast_to(sid.astype(jnp.float32), held_sid.shape[1:])
    sides = side_copies()
    for copy in sides:
        copy.start()
    acc[...] = jnp.zeros_like(acc)

    def add(k, slot):
        for q in range(queries):
            acc[slot, q] += lax.dot_general(
                held_grad[slot, k],
                held_query[k, q],
                (((1,), (1,)), ((), ())),
                preferred_element_type=jnp.float32,
            )

    @pl.loop(0, chunks)
    def _(k):
        query_copy(k).wait()
        own_copy(k).wait()
        add(k, 0)
        far_copy(k).wait_recv()

        @pl.when(even)
        def _():
            relay_copy(k).start()

        add(k, 2)
        near_copy(k).wait_recv()
        add(k, 1)

    sides[1].wait_recv()
    sides[3].wait_recv()
    lanes = lax.broadcasted_iota(jnp.int32, (tokens, pad), 1).astype(jnp.float32)
    members = []
    for slot in range(3):
        ids = jnp.broadcast_to(held_sid[slot][0:1, :], (tokens, tokens)).T
        members.append((lanes == ids[:, 0:1]).astype(jnp.float32))
    rows = [jnp.zeros((1, pad), jnp.float32) for _ in range(queries)]
    for slot, ready in ((0, own_act.wait), (1, sides[0].wait_recv), (2, sides[2].wait_recv)):
        ready()
        act = held_act[slot].astype(jnp.float32)
        for q in range(queries):
            value = jnp.sum(acc[slot, q] * act, axis=1, keepdims=True)
            rows[q] = rows[q] + jnp.sum(value * members[slot], axis=0, keepdims=True)
    sub = lax.broadcasted_iota(jnp.int32, term_mine.shape, 0)
    mine = jnp.zeros(term_mine.shape, jnp.float32)
    for q in range(queries):
        mine = jnp.where(sub == q, jnp.broadcast_to(rows[q], term_mine.shape), mine)
    term_mine[...] = mine

    for d in range(1, count):
        term_copy(d).start()

    @pl.loop(0, chunks)
    def _(k):
        far_copy(k).wait_send()
        near_copy(k).wait_send()

    for copy in sides:
        copy.wait_send()

    def gather(d, total):
        term_copy(d).wait_recv()
        return total + term_got[d]

    total = lax.fori_loop(1, count, gather, term_mine[...])
    lane = lax.broadcasted_iota(jnp.int32, total.shape, 1)
    spot = lax.broadcasted_iota(jnp.int32, out_ref.shape, 1)
    result = jnp.zeros(out_ref.shape, jnp.float32)
    for s in range(SEQS_DEV):
        picked = jnp.sum(
            jnp.where(lane == me * SEQS_DEV + s, total, 0.0), axis=1, keepdims=True
        )
        result = jnp.where(
            spot == s, jnp.broadcast_to(picked[:queries], out_ref.shape), result
        )
    out_ref[...] = result

    @pl.loop(1, count)
    def _(d):
        term_copy(d).wait_send()


def local(activations, out_grads, query_grad, segment_ids, sequence_ids):
    count = lax.axis_size("seq")
    queries, band, width = query_grad.shape
    tokens = out_grads.shape[0]
    chunk = math.gcd(width, 1024)
    chunks = width // chunk
    pad = -(-SEQS_DEV * count // 128) * 128
    sub = -(-queries // 8) * 8
    dma = pltpu.SemaphoreType.DMA
    whole = pl.BlockSpec(memory_space=pl.ANY)
    return pl.pallas_call(
        functools.partial(kernel, count, chunk),
        out_shape=jax.ShapeDtypeStruct((queries, SEQS_DEV), jnp.float32),
        in_specs=[
            whole,
            whole,
            whole,
            whole,
            whole,
        ],
        out_specs=pl.BlockSpec(memory_space=pltpu.VMEM),
        scratch_shapes=[
            pltpu.VMEM((chunks, queries, band, chunk), jnp.bfloat16),
            pltpu.VMEM((3, chunks, tokens, chunk), jnp.bfloat16),
            pltpu.VMEM((3, tokens, band), jnp.bfloat16),
            pltpu.VMEM((3, 8, tokens), jnp.float32),
            pltpu.VMEM(segment_ids.shape, jnp.int32),
            pltpu.SMEM(sequence_ids.shape, jnp.int32),
            pltpu.VMEM((3, queries, tokens, band), jnp.float32),
            pltpu.VMEM((sub, pad), jnp.float32),
            pltpu.VMEM((count, sub, pad), jnp.float32),
            dma((chunks,)),
            dma((chunks,)),
            dma,
            dma((2,)),
            dma((chunks,)),
            dma((chunks,)),
            dma((chunks,)),
            dma((chunks,)),
            dma((4,)),
            dma((4,)),
            dma((count,)),
            dma((count,)),
        ],
        compiler_params=pltpu.CompilerParams(
            collective_id=0, has_side_effects=True, vmem_limit_bytes=56 * 1024 * 1024
        ),
        cost_estimate=pl.CostEstimate(
            flops=6 * queries * tokens * band * width,
            bytes_accessed=2 * queries * band * width,
            transcendentals=0,
        ),
    )(activations, out_grads, query_grad, segment_ids, sequence_ids)


def solution(mesh):
    placed = (
        P(("groups", "seq"), None),
        P(("groups", "seq"), None),
        P(None, ("groups", "seq"), None),
        P(("groups", "seq"), None),
        P(("groups", "seq"), None),
    )
    return jax.shard_map(
        local, mesh=mesh, in_specs=placed, out_specs=P(None, ("groups", "seq")), check_vma=False
    )
```

```python
import functools
import math

import jax
import jax.numpy as jnp
from jax import lax
from jax.experimental import pallas as pl
from jax.experimental.pallas import tpu as pltpu
from jax.sharding import PartitionSpec as P

SEGS = 4
SEQS_DEV = 2
MESH = pl.DeviceIdType.MESH


def kernel(
    count,
    chunk,
    act_ref,
    grad_ref,
    query_ref,
    seg_ref,
    seq_ref,
    out_ref,
    held_query,
    held_grad,
    held_act,
    held_sid,
    held_seg,
    held_seq,
    acc,
    term_mine,
    term_got,
    query_sem,
    own_sem,
    act_sem,
    id_sem,
    far_send,
    far_recv,
    near_send,
    near_recv,
    side_send,
    side_recv,
    term_send,
    term_recv,
):
    group = lax.axis_index("groups")
    me = lax.axis_index("seq")
    queries, band, width = query_ref.shape
    tokens = grad_ref.shape[0]
    chunks = width // chunk
    pad = term_mine.shape[1]
    even = lax.rem(me, 2) == 0
    back1 = lax.rem(me + count - 1, count)
    back2 = lax.rem(me + count - 2, count)
    ahead1 = lax.rem(me + 1, count)

    def columns(owner):
        return act_ref.at[:, pl.ds(pl.multiple_of(owner * band, band), band)]

    def span(k):
        return pl.ds(pl.multiple_of(k * chunk, chunk), chunk)

    def query_copy(k):
        return pltpu.make_async_copy(
            query_ref.at[:, :, span(k)], held_query.at[k], query_sem.at[k]
        )

    def own_copy(k):
        return pltpu.make_async_copy(grad_ref.at[:, span(k)], held_grad.at[0, k], own_sem.at[k])

    def far_copy(k):
        return pltpu.make_async_remote_copy(
            src_ref=grad_ref.at[:, span(k)],
            dst_ref=held_grad.at[2, k],
            send_sem=far_send.at[k],
            recv_sem=far_recv.at[k],
            device_id=(group, back2),
            device_id_type=MESH,
        )

    def near_copy(k):
        return pltpu.make_async_remote_copy(
            src_ref=grad_ref.at[:, span(k)],
            dst_ref=held_grad.at[1, k],
            send_sem=near_send.at[k],
            recv_sem=near_recv.at[k],
            device_id=(group, back1),
            device_id_type=MESH,
        )

    def relay_copy(k):
        return pltpu.make_async_remote_copy(
            src_ref=held_grad.at[2, k],
            dst_ref=held_grad.at[1, k],
            send_sem=near_send.at[k],
            recv_sem=near_recv.at[k],
            device_id=(group, ahead1),
            device_id_type=MESH,
        )

    def side_copies():
        made = []
        for slot, target in ((1, back1), (2, back2)):
            for kind, source, place in (
                (0, columns(target), held_act.at[slot]),
                (1, held_sid.at[0], held_sid.at[slot]),
            ):
                index = 2 * (slot - 1) + kind
                made.append(
                    pltpu.make_async_remote_copy(
                        src_ref=source,
                        dst_ref=place,
                        send_sem=side_send.at[index],
                        recv_sem=side_recv.at[index],
                        device_id=(group, target),
                        device_id_type=MESH,
                    )
                )
        return made

    def term_copy(d):
        return pltpu.make_async_remote_copy(
            src_ref=term_mine,
            dst_ref=term_got.at[d],
            send_sem=term_send.at[d],
            recv_sem=term_recv.at[d],
            device_id=(group, lax.rem(me + d, count)),
            device_id_type=MESH,
        )

    barrier = pltpu.get_barrier_semaphore()
    for d in range(1, count):
        pl.semaphore_signal(
            barrier,
            inc=1,
            device_id=(group, lax.rem(me + d, count)),
            device_id_type=MESH,
        )
    seg_copy = pltpu.make_async_copy(seg_ref, held_seg, id_sem.at[0])
    seq_copy = pltpu.make_async_copy(seq_ref, held_seq, id_sem.at[1])
    seg_copy.start()
    seq_copy.start()
    pl.semaphore_wait(barrier, count - 1)

    @pl.loop(0, chunks)
    def _(k):
        far_copy(k).start()

    @pl.when(lax.rem(me, 2) == 1)
    def _():
        @pl.loop(0, chunks)
        def _(k):
            near_copy(k).start()

    @pl.loop(0, chunks)
    def _(k):
        query_copy(k).start()
        own_copy(k).start()

    own_act = pltpu.make_async_copy(columns(me), held_act.at[0], act_sem)
    own_act.start()
    seg_copy.wait()
    seq_copy.wait()
    sid = jnp.zeros((1, tokens), jnp.int32)
    for s in range(SEGS):
        sid = sid + jnp.where(held_seg[...] == s, held_seq[0, s], 0)
    held_sid[0] = jnp.broadcast_to(sid.astype(jnp.float32), held_sid.shape[1:])
    sides = side_copies()
    for copy in sides[1::2] + sides[0::2]:
        copy.start()
    acc[...] = jnp.zeros_like(acc)

    def add(k, slot):
        for q in range(queries):
            acc[slot, q] += lax.dot_general(
                held_grad[slot, k],
                held_query[k, q],
                (((1,), (1,)), ((), ())),
                preferred_element_type=jnp.float32,
            )

    @pl.loop(0, chunks)
    def _(k):
        query_copy(k).wait()
        own_copy(k).wait()
        add(k, 0)
        far_copy(k).wait_recv()

        @pl.when(even)
        def _():
            relay_copy(k).start()

        add(k, 2)
        near_copy(k).wait_recv()
        add(k, 1)

    sides[1].wait_recv()
    sides[3].wait_recv()
    lanes = lax.broadcasted_iota(jnp.int32, (tokens, pad), 1).astype(jnp.float32)
    members = []
    for slot in range(3):
        ids = jnp.broadcast_to(held_sid[slot][0:1, :], (tokens, tokens)).T
        members.append((lanes == ids[:, 0:1]).astype(jnp.float32))
    rows = [jnp.zeros((1, pad), jnp.float32) for _ in range(queries)]
    for slot, ready in ((0, own_act.wait), (1, sides[0].wait_recv), (2, sides[2].wait_recv)):
        ready()
        act = held_act[slot].astype(jnp.float32)
        for q in range(queries):
            value = jnp.sum(acc[slot, q] * act, axis=1, keepdims=True)
            rows[q] = rows[q] + jnp.sum(value * members[slot], axis=0, keepdims=True)
    sub = lax.broadcasted_iota(jnp.int32, term_mine.shape, 0)
    mine = jnp.zeros(term_mine.shape, jnp.float32)
    for q in range(queries):
        mine = jnp.where(sub == q, jnp.broadcast_to(rows[q], term_mine.shape), mine)
    term_mine[...] = mine

    for d in range(1, count):
        term_copy(d).start()

    @pl.loop(0, chunks)
    def _(k):
        far_copy(k).wait_send()
        near_copy(k).wait_send()

    for copy in sides:
        copy.wait_send()

    def gather(d, total):
        term_copy(d).wait_recv()
        return total + term_got[d]

    total = lax.fori_loop(1, count, gather, term_mine[...])
    lane = lax.broadcasted_iota(jnp.int32, total.shape, 1)
    spot = lax.broadcasted_iota(jnp.int32, out_ref.shape, 1)
    result = jnp.zeros(out_ref.shape, jnp.float32)
    for s in range(SEQS_DEV):
        picked = jnp.sum(
            jnp.where(lane == me * SEQS_DEV + s, total, 0.0), axis=1, keepdims=True
        )
        result = jnp.where(
            spot == s, jnp.broadcast_to(picked[:queries], out_ref.shape), result
        )
    out_ref[...] = result

    @pl.loop(1, count)
    def _(d):
        term_copy(d).wait_send()


def local(activations, out_grads, query_grad, segment_ids, sequence_ids):
    count = lax.axis_size("seq")
    queries, band, width = query_grad.shape
    tokens = out_grads.shape[0]
    chunk = math.gcd(width, 1024)
    chunks = width // chunk
    pad = -(-SEQS_DEV * count // 128) * 128
    sub = -(-queries // 8) * 8
    dma = pltpu.SemaphoreType.DMA
    whole = pl.BlockSpec(memory_space=pl.ANY)
    return pl.pallas_call(
        functools.partial(kernel, count, chunk),
        out_shape=jax.ShapeDtypeStruct((queries, SEQS_DEV), jnp.float32),
        in_specs=[
            whole,
            whole,
            whole,
            whole,
            whole,
        ],
        out_specs=pl.BlockSpec(memory_space=pltpu.VMEM),
        scratch_shapes=[
            pltpu.VMEM((chunks, queries, band, chunk), jnp.bfloat16),
            pltpu.VMEM((3, chunks, tokens, chunk), jnp.bfloat16),
            pltpu.VMEM((3, tokens, band), jnp.bfloat16),
            pltpu.VMEM((3, 8, tokens), jnp.float32),
            pltpu.VMEM(segment_ids.shape, jnp.int32),
            pltpu.SMEM(sequence_ids.shape, jnp.int32),
            pltpu.VMEM((3, queries, tokens, band), jnp.float32),
            pltpu.VMEM((sub, pad), jnp.float32),
            pltpu.VMEM((count, sub, pad), jnp.float32),
            dma((chunks,)),
            dma((chunks,)),
            dma,
            dma((2,)),
            dma((chunks,)),
            dma((chunks,)),
            dma((chunks,)),
            dma((chunks,)),
            dma((4,)),
            dma((4,)),
            dma((count,)),
            dma((count,)),
        ],
        compiler_params=pltpu.CompilerParams(
            collective_id=0, has_side_effects=True, vmem_limit_bytes=56 * 1024 * 1024
        ),
        cost_estimate=pl.CostEstimate(
            flops=6 * queries * tokens * band * width,
            bytes_accessed=2 * queries * band * width,
            transcendentals=0,
        ),
    )(activations, out_grads, query_grad, segment_ids, sequence_ids)


def solution(mesh):
    placed = (
        P(("groups", "seq"), None),
        P(("groups", "seq"), None),
        P(None, ("groups", "seq"), None),
        P(("groups", "seq"), None),
        P(("groups", "seq"), None),
    )
    return jax.shard_map(
        local, mesh=mesh, in_specs=placed, out_specs=P(None, ("groups", "seq")), check_vma=False
    )
```
